32 devices in a mesh: ens: 2 (over y), row: 4 (over z), col: 2 (over x), chan: 2 (over core).
Axes of the slice: x: 2, y: 2, z: 4, core: 2. Of those that a mesh axis runs over, the one named last changes fastest.
Arguments:
- latent: float32 [4, 12, 32, 256], P('ens', None, 'row', 'col'), parts along dimension 0, may hold values from -6 to 6
- fresh_noise: float32 [4, 12, 32, 256], P('ens', None, 'row', 'col'), parts along dimension 0, may hold values from -6 to 6
- step_index: int32 [4], P('ens'), parts along dimension 0, may hold values from 0 to 11
- coarse: float32 [24, 4, 32], P('ens', None, 'col'), parts along dimension 0, may hold values from -6 to 6
- weight_in: bfloat16 [9, 256, 24], replicated, may hold values from -0.4375 to 0.4375
- bias_in: float32 [256], replicated, may hold values from -4 to 4
- weight_noise: float32 [256], replicated, may hold values from -4 to 4
- weight_mid: bfloat16 [9, 256, 256], P(None, 'chan'), may hold values from -0.125 to 0.125
- bias_mid: float32 [256], P('chan'), may hold values from -4 to 4
- weight_out: bfloat16 [12, 256], P(None, 'chan'), may hold values from -0.375 to 0.375
Outputs:
- fine_field: float32 [4, 12, 32, 256], P('ens', None, 'row', 'col'), parts along dimension 0
- next_latent: float32 [4, 12, 32, 256], P('ens', None, 'row', 'col'), parts along dimension 0
The draws below stay inside these ranges and needn't reach their ends.
There are 2 independent parts, one for each index of `ens`. The reference program is written for one: setup_inputs(seed, part) draws one part's arguments, and reference() takes and returns one part's arrays. A program takes and returns all parts, laid end to end along the dimension named above; an argument that names none is the same for every part. Nothing has to cross between parts.
Inputs may be any that keep to these rules, and one draw needn't show every extreme that they name: `step_index`: each sample's position in the noise plan of 18 steps.
All inputs are finite; a program needn't handle non-finite values.
Results may differ from the reference program's by a relative error of at most 0.0024.
Values may be sent and summed in bfloat16 or wider, within the bound.
A program may use at most 64 MiB of HBM per device.

```python
import jax
import jax.numpy as jnp
from jax import lax

CC = 12
HID = 256
S = 2
STEPS = 18
FACTOR = 8
TH = 8
H = 32
W = 256
HC = 4
WC = 32


def level_of(key, shape, pieces, least, high):
    loudness = 1.0
    for dim, parts in pieces:
        draws = jax.random.uniform(jax.random.fold_in(jax.random.fold_in(key, 6), dim), (parts,), jnp.float32, least / len(pieces), high / len(pieces))
        loudness = loudness * jnp.repeat(jnp.exp(draws), shape[dim] // parts).reshape((-1,) + (1,) * (len(shape) - 1 - dim))
    return loudness


def normal_values(stream_key, shape, scale, reach, pieces=(), held_as=jnp.bfloat16):
    entries = jax.random.normal(stream_key, shape, jnp.float32) * scale
    if len(pieces) > 0:
        entries = level_of(stream_key, shape, pieces, -0.22, 0.18) * entries
    return jnp.clip(entries, min=-reach, max=reach).astype(held_as)


def setup_inputs(seed: int = 0, part: int = 0) -> dict:
    keys = jax.random.split(jax.random.key(seed), 11)
    part_splits = jax.random.split(jax.random.fold_in(keys[10], part), 11)
    latent = normal_values(part_splits[0], (S, CC, H, W), 1.0, 6.0, ((2, 4), (3, 2)), jnp.float32)
    fresh_noise = normal_values(part_splits[1], (S, CC, H, W), 1.0, 6.0, ((2, 4), (3, 2)), jnp.float32)
    step_index = jax.random.randint(part_splits[2], (S,), 0, 12).astype(jnp.int32)
    coarse = normal_values(part_splits[3], (CC, HC, WC), 1.0, 6.0, ((2, 2),), jnp.float32)
    weight_in = normal_values(keys[4], (9, HID, 2 * CC), (18 * CC) ** -0.5, 0.4375)
    bias_in = normal_values(keys[5], (HID,), 1.0, 4.0, (), jnp.float32)
    weight_noise = normal_values(keys[6], (HID,), 1.0, 4.0, (), jnp.float32)
    weight_mid = normal_values(keys[7], (9, HID, HID), (9 * HID) ** -0.5, 0.125, ((1, 2),))
    bias_mid = normal_values(keys[8], (HID,), 1.0, 4.0, ((0, 2),), jnp.float32)
    weight_out = normal_values(keys[9], (CC, HID), HID ** -0.5, 0.375, ((1, 2),))
    return dict(latent=latent, fresh_noise=fresh_noise, step_index=step_index, coarse=coarse, weight_in=weight_in, bias_in=bias_in, weight_noise=weight_noise, weight_mid=weight_mid, bias_mid=bias_mid, weight_out=weight_out)


sigma_data = 0.5
sigma_high = 80.0
sigma_low = 0.002
rho_power = 7.0

def blend_matrix(fine_index, coarse_index, coarse_count, factor):
    twice_pos = 2 * fine_index + 1 - factor
    lower_cell = twice_pos // (2 * factor)
    fraction = (twice_pos - lower_cell * 2 * factor).astype(jnp.float32) / (2.0 * factor)
    before = lower_cell < 0
    fraction = jnp.where(before, 0.0, fraction)
    lower_clip = jnp.clip(lower_cell, 0, coarse_count - 1)
    upper_clip = jnp.clip(lower_cell + 1, 0, coarse_count - 1)
    lower_hit = (lower_clip[:, None] == coarse_index[None, :]).astype(jnp.float32)
    upper_hit = (upper_clip[:, None] == coarse_index[None, :]).astype(jnp.float32)
    return (1.0 - fraction)[:, None] * lower_hit + fraction[:, None] * upper_hit

def noise_level(position):
    top_root = sigma_high ** (1.0 / rho_power)
    bottom_root = sigma_low ** (1.0 / rho_power)
    along = position.astype(jnp.float32) / (STEPS - 1)
    return (top_root + along * (bottom_root - top_root)) ** rho_power

def conv_valid(source, weight, out_rows, out_cols):
    total = None
    for offset_row in range(3):
        for offset_col in range(3):
            window = source[:, :, offset_row:offset_row + out_rows, offset_col:offset_col + out_cols]
            term = jnp.einsum('oi,siyx->soyx', weight[3 * offset_row + offset_col].astype(jnp.float32), window.astype(jnp.float32), precision=lax.Precision.HIGHEST)
            total = term if total is None else total + term
    return total

def reference(latent, fresh_noise, step_index, coarse, weight_in, bias_in, weight_noise, weight_mid, bias_mid, weight_out):
    samples, channels, height, width = latent.shape
    coarse_rows = coarse.shape[1]
    coarse_cols = coarse.shape[2]
    rows_matrix = blend_matrix(jnp.arange(height, dtype=jnp.int32), jnp.arange(coarse_rows, dtype=jnp.int32), coarse_rows, FACTOR)
    cols_matrix = blend_matrix(jnp.arange(width, dtype=jnp.int32), jnp.arange(coarse_cols, dtype=jnp.int32), coarse_cols, FACTOR)
    mean_up = jnp.einsum('yh,khw,xw->kyx', rows_matrix, coarse, cols_matrix, precision=lax.Precision.HIGHEST)
    noise_now = noise_level(step_index)
    noise_next = noise_level(step_index + 1)
    inputs = jnp.concatenate([latent, jnp.broadcast_to(mean_up[None], (samples,) + mean_up.shape)], axis=1).astype(jnp.bfloat16)
    padded = jnp.pad(inputs, ((0, 0), (0, 0), (2, 2), (2, 2)))
    conditioning = bias_in[None, :, None, None] + (jnp.log(noise_now) / 4.0)[:, None, None, None] * weight_noise[None, :, None, None]
    band_rows = TH
    band_count = height // band_rows

    def one_band(band_index):
        start_row = band_index * band_rows
        source = lax.dynamic_slice_in_dim(padded, start_row, band_rows + 4, 2)
        hidden = jax.nn.silu(conv_valid(source, weight_in, band_rows + 2, width + 2) + conditioning)
        global_rows = start_row - 1 + jnp.arange(band_rows + 2, dtype=jnp.int32)
        global_cols = -1 + jnp.arange(width + 2, dtype=jnp.int32)
        inside = ((global_rows >= 0) & (global_rows < height))[:, None] & ((global_cols >= 0) & (global_cols < width))[None, :]
        hidden = jnp.where(inside, hidden, 0.0).astype(jnp.bfloat16)
        middle = jax.nn.silu(conv_valid(hidden, weight_mid, band_rows, width) + bias_mid[None, :, None, None]).astype(jnp.bfloat16)
        return jnp.einsum('ko,soyx->skyx', weight_out.astype(jnp.float32), middle.astype(jnp.float32), precision=lax.Precision.HIGHEST)
    bands = lax.map(one_band, jnp.arange(band_count, dtype=jnp.int32))
    network = jnp.transpose(bands, (1, 2, 0, 3, 4)).reshape(samples, channels, height, width)
    scale_now = jnp.sqrt(noise_now * noise_now + sigma_data * sigma_data)
    skip_coef = sigma_data * sigma_data / (noise_now * noise_now + sigma_data * sigma_data)
    out_coef = sigma_data * noise_now / scale_now
    denoised = (skip_coef * scale_now)[:, None, None, None] * latent + out_coef[:, None, None, None] * network
    fine_field = mean_up[None] + denoised
    scale_next = jnp.sqrt(noise_next * noise_next + sigma_data * sigma_data)
    next_latent = (denoised + noise_next[:, None, None, None] * fresh_noise) / scale_next[:, None, None, None]
    return (fine_field, next_latent)
```

```python
import functools

import jax
import jax.numpy as jnp
from jax import lax
from jax.experimental import pallas as pl
from jax.experimental.pallas import tpu as pltpu
from jax.sharding import PartitionSpec as P

STEPS = 18
sigma_data = 0.5
sigma_high = 80.0
sigma_low = 0.002
rho_power = 7.0
top_root = sigma_high ** (1.0 / rho_power)
bottom_root = sigma_low ** (1.0 / rho_power)

MESH = pl.DeviceIdType.MESH
UP, DOWN, LEFT, RIGHT, UL, UR, DL, DR = range(8)
STEP = {
    UP: (-1, 0), DOWN: (1, 0), LEFT: (0, -1), RIGHT: (0, 1),
    UL: (-1, -1), UR: (-1, 1), DL: (1, -1), DR: (1, 1),
}
BACK = {UP: DOWN, DOWN: UP, LEFT: RIGHT, RIGHT: LEFT, UL: DR, DR: UL, UR: DL, DL: UR}
COARSE = {LEFT: 8, RIGHT: 9}
WEIGHTS, AUX, NET, OWN = 10, 11, 12, 13
HALO = 2
GROUP = 24
BLOCK = 80
EDGE = 8


def silu(v):
    half = 0.5 * v
    return half * (1.0 + jnp.tanh(half))


def iota(shape, dim):
    return lax.broadcasted_iota(jnp.int32, shape, dim)


def blend(position, index, count, factor):
    u = (position + 0.5) / factor - 0.5
    cell = jnp.floor(u)
    fraction = jnp.where(u < 0.0, 0.0, u - cell)
    low = jnp.maximum(cell, 0.0)
    high = jnp.minimum(jnp.maximum(cell + 1.0, 0.0), count - 1.0)
    low_hit = jnp.where(low == index, 1.0 - fraction, 0.0)
    high_hit = jnp.where(high == index, fraction, 0.0)
    return low_hit + high_hit


def base_level(step):
    return top_root + step / (STEPS - 1) * (bottom_root - top_root)


def power7(b):
    b2 = b * b
    return b2 * b2 * b2 * b


def column(row_vector):
    n = row_vector.shape[1]
    parts = [
        jnp.transpose(jnp.broadcast_to(row_vector[:, a : a + 128], (128, 128)))
        for a in range(0, n, 128)
    ]
    return parts[0] if len(parts) == 1 else jnp.concatenate(parts, axis=0)


def kernel(
    sizes,
    latent_ref, fresh_ref, step_ref, coarse_ref, weight_in_ref, bias_in_ref, weight_noise_ref,
    weight_mid_ref, bias_mid_ref, weight_out_ref,
    fine_ref, next_ref,
    center, packs, coarse_t, coarse_st, aux, w_mid, w_in_t, xj, xe, hc, net, means, cond, bias_mid_col,
    send_sem, recv_sem, own_sem,
):
    n_row, n_col, factor = sizes
    samples, channels, rows, cols = latent_ref.shape
    coarse_rows, coarse_here = coarse_ref.shape[1], coarse_ref.shape[2]
    hidden = weight_in_ref.shape[2]
    half_hidden = hidden // 2
    ext = rows + 2 * HALO
    row_place, col_place = lax.axis_index("row"), lax.axis_index("col")
    me = lax.axis_index("chan")
    other = 1 - me

    def exists(d):
        dr, dc = STEP[d]
        conds = []
        if dr < 0:
            conds.append(row_place > 0)
        if dr > 0:
            conds.append(row_place < n_row - 1)
        if dc < 0:
            conds.append(col_place > 0)
        if dc > 0:
            conds.append(col_place < n_col - 1)
        return conds[0] if len(conds) == 1 else jnp.logical_and(*conds)

    def target(d):
        return {"row": row_place + STEP[d][0], "col": col_place + STEP[d][1]}

    center[...] = jnp.zeros_like(center)
    packs[...] = jnp.zeros_like(packs)
    coarse_t[...] = jnp.zeros_like(coarse_t)

    barrier = pltpu.get_barrier_semaphore()
    pl.semaphore_signal(barrier, inc=1, device_id={"chan": other}, device_id_type=MESH)
    for d in range(8):
        @pl.when(exists(d))
        def _(d=d):
            pl.semaphore_signal(barrier, inc=1, device_id=target(d), device_id_type=MESH)

    half = pl.ds(pl.multiple_of(me * half_hidden, half_hidden), half_hidden)
    own_weights = pltpu.make_async_copy(weight_mid_ref, w_mid.at[:, half, :], own_sem)
    own_weights.start()

    lane = iota((GROUP, cols), 1)
    pack = jnp.zeros((GROUP, cols), jnp.float32)
    for y in range(rows):
        center[HALO + y, 0:channels, :] = latent_ref[me, :, y, :]
        v = center[HALO + y]
        for source, place in ((cols - 1, y), (cols - 2, 16 + y), (0, cols - 1 - y), (1, cols - 17 - y)):
            pack = jnp.where(lane == place, pltpu.roll(v, (place - source) % cols, 1), pack)
    packs[8] = pack
    coarse_st[...] = jnp.zeros_like(coarse_st)
    for h in range(coarse_rows):
        start = h * GROUP + channels
        coarse_st[start : start + channels, 0:coarse_here] = coarse_ref[:, h, :]
    turned = jnp.transpose(coarse_st[...])
    coarse_t[EDGE : EDGE + coarse_here, :] = turned[0:coarse_here, :]
    aux[me] = jnp.zeros(aux.shape[1:], jnp.float32)
    aux[me, 0:channels, :] = weight_out_ref[...].astype(jnp.float32)
    aux[me, 16:17, :] = bias_mid_ref[...]

    up_ok = jnp.where(row_place > 0, 1, 0)
    down_ok = jnp.where(row_place < n_row - 1, 1, 0)
    left_ok = jnp.where(col_place > 0, 1, 0)
    right_ok = jnp.where(col_place < n_col - 1, 1, 0)
    links = (1 + up_ok + down_ok) * (1 + left_ok + right_ok)
    pl.semaphore_wait(barrier, links)

    def remote(src, dst, sem, where, arrive=None):
        return pltpu.make_async_remote_copy(
            src_ref=src, dst_ref=dst, send_sem=send_sem.at[sem],
            recv_sem=recv_sem.at[sem if arrive is None else arrive],
            device_id=where, device_id_type=MESH,
        )

    def message(d):
        arrive = BACK[d]
        if d == UP:
            src, dst = center.at[HALO : 2 * HALO], center.at[rows + HALO : rows + 2 * HALO]
        elif d == DOWN:
            src, dst = center.at[rows : rows + HALO], center.at[0:HALO]
        else:
            src, dst = packs.at[8], packs.at[arrive]
        return remote(src, dst, d, target(d), arrive)

    def coarse_message(d):
        if d == LEFT:
            src, dst = coarse_t.at[EDGE : 2 * EDGE], coarse_t.at[EDGE + coarse_here : 2 * EDGE + coarse_here]
        else:
            src, dst = coarse_t.at[coarse_here : EDGE + coarse_here], coarse_t.at[0:EDGE]
        return remote(src, dst, COARSE[d], target(d), COARSE[BACK[d]])

    for d in (LEFT, RIGHT):
        @pl.when(exists(d))
        def _(d=d):
            coarse_message(d).start()
    for d in (UL, UR, DL, DR, UP, DOWN, LEFT, RIGHT):
        @pl.when(exists(d))
        def _(d=d):
            message(d).start()
    send_aux = remote(aux.at[me], aux.at[me], AUX, {"chan": other})
    send_aux.start()
    send_weights = remote(weight_mid_ref, w_mid.at[:, half, :], WEIGHTS, {"chan": other})
    send_weights.start()

    w_in_t[...] = jnp.zeros_like(w_in_t)
    for i in range(3):
        for j in range(3):
            start = BLOCK * i + GROUP * j
            w_in_t[start : start + GROUP, :] = weight_in_ref[3 * i + j].astype(jnp.float32)
    w_first = jnp.transpose(w_in_t[...]).astype(jnp.bfloat16)[:, 0 : 3 * BLOCK]
    step_here = jnp.full((1, hidden), step_ref[me].astype(jnp.float32), jnp.float32)
    log_noise = rho_power * jnp.log(base_level(step_here))
    cond[...] = column(bias_in_ref[...] + log_noise / 4.0 * weight_noise_ref[...])

    n_coarse = coarse_t.shape[0]
    index = (iota((n_coarse, cols), 0) + (col_place * coarse_here - EDGE)).astype(jnp.float32)
    x_here = iota((n_coarse, cols), 1)
    x_edge = jnp.where(x_here < cols // 2, -2, cols - 1)
    width = n_col * cols
    tables = []
    for x in [x_here + j - 1 for j in range(3)] + [x_edge + j for j in range(3)]:
        x = x + col_place * cols
        weight = blend(x.astype(jnp.float32), index, float(n_col * coarse_here), float(factor))
        tables.append(jnp.where((x >= 0) & (x < width), weight, 0.0))
    table = jnp.concatenate(tables, axis=1)
    y_ext = iota((16, 128), 0) + (row_place * rows - HALO)
    y_valid = (y_ext >= 0) & (y_ext < n_row * rows)
    row_weights = [
        jnp.where(y_valid, blend(y_ext.astype(jnp.float32), float(h), float(coarse_rows), float(factor)), 0.0)
        for h in range(coarse_rows)
    ]

    for d in (LEFT, RIGHT):
        @pl.when(exists(d))
        def _(d=d):
            coarse_message(BACK[d]).wait_recv()
    across = lax.dot_general(
        coarse_t[...], table, (((0,), (0,)), ((), ())),
        precision=lax.Precision.HIGHEST, preferred_element_type=jnp.float32,
    )
    means[...] = across

    def mean_rows(r, which):
        total = None
        for h in range(coarse_rows):
            term = row_weights[h][r : r + 1, :] * means[h * GROUP : (h + 1) * GROUP, which * cols : (which + 1) * cols]
            total = term if total is None else total + term
        return total

    for d in (UP, DOWN, LEFT, RIGHT, UL, UR, DL, DR):
        @pl.when(exists(d))
        def _(d=d):
            message(BACK[d]).wait_recv()

    zeros = jnp.zeros((BLOCK - 3 * GROUP, cols), jnp.float32)
    for r in range(ext):
        if r < HALO:
            from_left, from_right, y = UL, UR, rows - HALO + r
        elif r < rows + HALO:
            from_left, from_right, y = LEFT, RIGHT, r - HALO
        else:
            from_left, from_right, y = DL, DR, r - rows - HALO
        pack_left, pack_right = packs[from_left], packs[from_right]
        near = jnp.where(
            lane < cols // 2, pltpu.roll(pack_left, (-y) % cols, 1), pltpu.roll(pack_right, y, 1)
        )
        far = jnp.where(
            lane < cols // 2, pltpu.roll(pack_left, (-16 - y) % cols, 1), pltpu.roll(pack_right, 16 + y, 1)
        )
        own = center[r]
        shifted = [
            jnp.where(lane == 0, near, pltpu.roll(own, 1, 1)),
            own,
            jnp.where(lane == cols - 1, near, pltpu.roll(own, cols - 1, 1)),
        ]
        edges = [
            jnp.where(lane < cols // 2, far, own),
            near,
            jnp.where(lane < cols // 2, own, far),
        ]
        here = slice(r * cols, (r + 1) * cols)
        xj[:, here] = jnp.concatenate(
            [shifted[j] + mean_rows(r, j) for j in range(3)] + [zeros], axis=0
        ).astype(jnp.bfloat16)
        xe[:, here] = jnp.concatenate(
            [edges[j] + mean_rows(r, 3 + j) for j in range(3)] + [zeros], axis=0
        ).astype(jnp.bfloat16)

    conditioning = cond[...]
    wide_lane = iota((hidden, cols), 1)
    side_ok = jnp.where(
        wide_lane < cols // 2, left_ok.astype(jnp.float32), right_ok.astype(jnp.float32)
    )
    for y in range(0, rows + 2, 2):
        def taps(ref):
            return jnp.concatenate(
                [ref[:, (y + i) * cols : (y + i + 2) * cols] for i in range(3)], axis=0
            )
        main = jnp.dot(w_first, taps(xj), preferred_element_type=jnp.float32)
        edge = jnp.dot(w_first, taps(xe), preferred_element_type=jnp.float32)
        for k in range(2):
            part = slice(k * cols, (k + 1) * cols)
            value = silu(main[:, part] + conditioning)
            side = silu(edge[:, part] + conditioning) * side_ok
            if y + k == 0:
                value, side = value * up_ok.astype(jnp.float32), side * up_ok.astype(jnp.float32)
            if y + k == rows + 1:
                value, side = value * down_ok.astype(jnp.float32), side * down_ok.astype(jnp.float32)
            before = jnp.where(wide_lane == 0, side, pltpu.roll(value, 1, 1))
            after = jnp.where(wide_lane == cols - 1, side, pltpu.roll(value, cols - 1, 1))
            here = slice((y + k) * cols, (y + k + 1) * cols)
            hc[0:hidden, here] = before.astype(jnp.bfloat16)
            hc[hidden : 2 * hidden, here] = value.astype(jnp.bfloat16)
            hc[2 * hidden : 3 * hidden, here] = after.astype(jnp.bfloat16)

    send_aux.wait_recv()
    w_out = jnp.concatenate([aux[0, 0:16], aux[1, 0:16]], axis=1).astype(jnp.bfloat16)
    bias_mid_col[...] = column(jnp.concatenate([aux[0, 16:17], aux[1, 16:17]], axis=1))
    own_weights.wait()
    send_weights.wait_recv()
    bias_wide = jnp.concatenate([bias_mid_col[...]] * 2, axis=1)
    for y in range(0, rows, 2):
        total = None
        for i in range(3):
            w = jnp.concatenate([w_mid[3 * i + j] for j in range(3)], axis=1)
            term = jnp.dot(
                w, hc[:, (y + i) * cols : (y + i + 2) * cols], preferred_element_type=jnp.float32
            )
            total = term if total is None else total + term
        middle = silu(total + bias_wide).astype(jnp.bfloat16)
        out = jnp.dot(w_out, middle, preferred_element_type=jnp.float32)
        for k in range(2):
            net[me, :, y + k, :] = out[0:channels, k * cols : (k + 1) * cols]
    send_net = remote(net.at[me], net.at[me], NET, {"chan": other})
    send_net.start()

    row_local = iota((rows, cols), 0) + row_place * rows
    out_weights = [
        blend(row_local.astype(jnp.float32), float(h), float(coarse_rows), float(factor))
        for h in range(coarse_rows)
    ]
    mean_out = []
    for c in range(channels):
        total = None
        for h in range(coarse_rows):
            at = h * GROUP + channels + c
            term = out_weights[h] * means[at : at + 1, cols : 2 * cols]
            total = term if total is None else total + term
        mean_out.append(total)

    def finish(s):
        step = jnp.full((rows, cols), step_ref[s].astype(jnp.float32), jnp.float32)
        now, later = power7(base_level(step)), power7(base_level(step + 1.0))
        variance = now * now + sigma_data * sigma_data
        scale_now = jnp.sqrt(variance)
        keep = sigma_data * sigma_data / variance * scale_now
        gain = sigma_data * now / scale_now
        shrink = 1.0 / jnp.sqrt(later * later + sigma_data * sigma_data)
        for c in range(channels):
            denoised = keep * latent_ref[s, c] + gain * net[s, c]
            fine_ref[s, c] = mean_out[c] + denoised
            next_ref[s, c] = (denoised + later * fresh_ref[s, c]) * shrink

    finish(me)
    send_net.wait_recv()
    finish(other)

    for d in range(8):
        @pl.when(exists(d))
        def _(d=d):
            message(d).wait_send()
    for d in (LEFT, RIGHT):
        @pl.when(exists(d))
        def _(d=d):
            coarse_message(d).wait_send()
    send_aux.wait_send()
    send_weights.wait_send()
    send_net.wait_send()


def on_device(
    latent, fresh_noise, step_index, coarse, weight_in, bias_in, weight_noise,
    weight_mid, bias_mid, weight_out,
):
    samples, channels, rows, cols = latent.shape
    coarse_rows, coarse_here = coarse.shape[1], coarse.shape[2]
    hidden = weight_in.shape[1]
    ext = rows + 2 * HALO
    stacked = -(-coarse_rows * GROUP // 128) * 128
    sizes = (lax.axis_size("row"), lax.axis_size("col"), cols // coarse_here)
    f32, bf16 = jnp.float32, jnp.bfloat16
    vmem = pl.BlockSpec(memory_space=pltpu.VMEM)
    specs = [vmem] * 10
    specs[2] = pl.BlockSpec(memory_space=pltpu.SMEM)
    specs[7] = pl.BlockSpec(memory_space=pl.ANY)
    return pl.pallas_call(
        functools.partial(kernel, sizes),
        out_shape=[jax.ShapeDtypeStruct(latent.shape, f32)] * 2,
        in_specs=specs,
        out_specs=[vmem, vmem],
        scratch_shapes=[
            pltpu.VMEM((ext, GROUP, cols), f32),
            pltpu.VMEM((9, GROUP, cols), f32),
            pltpu.VMEM((coarse_here + 2 * EDGE, stacked), f32),
            pltpu.VMEM((stacked, 128), f32),
            pltpu.VMEM((2, 24, hidden // 2), f32),
            pltpu.VMEM((9, hidden, hidden), bf16),
            pltpu.VMEM((256, hidden), f32),
            pltpu.VMEM((BLOCK, ext * cols), bf16),
            pltpu.VMEM((BLOCK, ext * cols), bf16),
            pltpu.VMEM((3 * hidden, (rows + 2) * cols), bf16),
            pltpu.VMEM((samples, channels, rows, cols), f32),
            pltpu.VMEM((stacked, 6 * cols), f32),
            pltpu.VMEM((hidden, cols), f32),
            pltpu.VMEM((hidden, cols), f32),
            pltpu.SemaphoreType.DMA((13,)),
            pltpu.SemaphoreType.DMA((13,)),
            pltpu.SemaphoreType.DMA,
        ],
        compiler_params=pltpu.CompilerParams(
            collective_id=0, has_side_effects=True, vmem_limit_bytes=40 * 1024 * 1024
        ),
        name="denoise_step",
    )(
        latent, fresh_noise, step_index, coarse, jnp.transpose(weight_in, (0, 2, 1)), bias_in.reshape(1, hidden),
        weight_noise.reshape(1, hidden), weight_mid, bias_mid.reshape(1, hidden // 2), weight_out,
    )


def solution(mesh):
    in_specs = (
        P("ens", None, "row", "col"),
        P("ens", None, "row", "col"),
        P("ens"),
        P("ens", None, "col"),
        P(),
        P(),
        P(),
        P(None, "chan", None),
        P("chan"),
        P(None, "chan"),
    )
    out_specs = (P("ens", None, "row", "col"), P("ens", None, "row", "col"))
    return jax.shard_map(
        on_device, mesh=mesh, in_specs=in_specs, out_specs=out_specs, check_vma=False
    )
```

```python
import functools

import jax
import jax.numpy as jnp
from jax import lax
from jax.experimental import pallas as pl
from jax.experimental.pallas import tpu as pltpu
from jax.sharding import PartitionSpec as P

STEPS = 18
sigma_data = 0.5
sigma_high = 80.0
sigma_low = 0.002
rho_power = 7.0
top_root = sigma_high ** (1.0 / rho_power)
bottom_root = sigma_low ** (1.0 / rho_power)

MESH = pl.DeviceIdType.MESH
UP, DOWN, LEFT, RIGHT, UL, UR, DL, DR = range(8)
STEP = {
    UP: (-1, 0), DOWN: (1, 0), LEFT: (0, -1), RIGHT: (0, 1),
    UL: (-1, -1), UR: (-1, 1), DL: (1, -1), DR: (1, 1),
}
BACK = {UP: DOWN, DOWN: UP, LEFT: RIGHT, RIGHT: LEFT, UL: DR, DR: UL, UR: DL, DL: UR}
COARSE = {LEFT: 8, RIGHT: 9}
WEIGHTS, AUX, NET = 10, 11, 12
HALO = 2
GROUP = 24
BLOCK = 80
EDGE = 8


def silu(v):
    half = 0.5 * v
    return half * (1.0 + jnp.tanh(half))


def iota(shape, dim):
    return lax.broadcasted_iota(jnp.int32, shape, dim)


def blend(position, index, count, factor):
    u = (position + 0.5) / factor - 0.5
    cell = jnp.floor(u)
    fraction = jnp.where(u < 0.0, 0.0, u - cell)
    low = jnp.maximum(cell, 0.0)
    high = jnp.minimum(jnp.maximum(cell + 1.0, 0.0), count - 1.0)
    low_hit = jnp.where(low == index, 1.0 - fraction, 0.0)
    high_hit = jnp.where(high == index, fraction, 0.0)
    return low_hit + high_hit


def base_level(step):
    return top_root + step / (STEPS - 1) * (bottom_root - top_root)


def power7(b):
    b2 = b * b
    return b2 * b2 * b2 * b


def column(row_vector):
    n = row_vector.shape[1]
    parts = [
        jnp.transpose(jnp.broadcast_to(row_vector[:, a : a + 128], (128, 128)))
        for a in range(0, n, 128)
    ]
    return parts[0] if len(parts) == 1 else jnp.concatenate(parts, axis=0)


def kernel(
    sizes,
    latent_hbm, fresh_hbm, step_hbm, coarse_hbm, weight_in_hbm, bias_in_hbm, weight_noise_hbm,
    weight_mid_ref, bias_mid_hbm, weight_out_hbm,
    fine_ref, next_ref,
    latent_ref, fresh_ref, step_ref, coarse_ref, weight_in_ref, bias_in_ref, weight_noise_ref,
    bias_mid_ref, weight_out_ref, load_sem,
    center, packs, coarse_t, coarse_st, aux, w_mid, w_in_t, xj, xe, hc, net, means, cond, bias_mid_col,
    send_sem, recv_sem, own_sem,
):
    n_row, n_col, factor = sizes
    samples, channels, rows, cols = latent_ref.shape
    coarse_rows, coarse_here = coarse_ref.shape[1], coarse_ref.shape[2]
    hidden = weight_in_ref.shape[2]
    half_hidden = hidden // 2
    ext = rows + 2 * HALO
    row_place, col_place = lax.axis_index("row"), lax.axis_index("col")
    me = lax.axis_index("chan")
    other = 1 - me

    def exists(d):
        dr, dc = STEP[d]
        conds = []
        if dr < 0:
            conds.append(row_place > 0)
        if dr > 0:
            conds.append(row_place < n_row - 1)
        if dc < 0:
            conds.append(col_place > 0)
        if dc > 0:
            conds.append(col_place < n_col - 1)
        return conds[0] if len(conds) == 1 else jnp.logical_and(*conds)

    def target(d):
        return {"row": row_place + STEP[d][0], "col": col_place + STEP[d][1]}

    loads = [
        pltpu.make_async_copy(src, dst, load_sem.at[n])
        for n, (src, dst) in enumerate((
            (latent_hbm, latent_ref), (coarse_hbm, coarse_ref), (weight_out_hbm, weight_out_ref),
            (bias_mid_hbm, bias_mid_ref), (weight_in_hbm, weight_in_ref), (step_hbm, step_ref),
            (bias_in_hbm, bias_in_ref), (weight_noise_hbm, weight_noise_ref), (fresh_hbm, fresh_ref),
        ))
    ]
    for load in loads:
        load.start()

    center[...] = jnp.zeros_like(center)
    packs[...] = jnp.zeros_like(packs)
    coarse_t[...] = jnp.zeros_like(coarse_t)

    barrier = pltpu.get_barrier_semaphore()
    pl.semaphore_signal(barrier, inc=1, device_id={"chan": other}, device_id_type=MESH)
    for d in range(8):
        @pl.when(exists(d))
        def _(d=d):
            pl.semaphore_signal(barrier, inc=1, device_id=target(d), device_id_type=MESH)

    half = pl.ds(pl.multiple_of(me * half_hidden, half_hidden), half_hidden)
    own_weights = pltpu.make_async_copy(weight_mid_ref, w_mid.at[:, half, :], own_sem)
    own_weights.start()

    for load in loads[0:4]:
        load.wait()
    lane = iota((GROUP, cols), 1)
    pack = jnp.zeros((GROUP, cols), jnp.float32)
    for y in range(rows):
        center[HALO + y, 0:channels, :] = latent_ref[me, :, y, :]
        v = center[HALO + y]
        for source, place in ((cols - 1, y), (cols - 2, 16 + y), (0, cols - 1 - y), (1, cols - 17 - y)):
            pack = jnp.where(lane == place, pltpu.roll(v, (place - source) % cols, 1), pack)
    packs[8] = pack
    coarse_st[...] = jnp.zeros_like(coarse_st)
    for h in range(coarse_rows):
        start = h * GROUP + channels
        coarse_st[start : start + channels, 0:coarse_here] = coarse_ref[:, h, :]
    turned = jnp.transpose(coarse_st[...])
    coarse_t[EDGE : EDGE + coarse_here, :] = turned[0:coarse_here, :]
    aux[me] = jnp.zeros(aux.shape[1:], jnp.float32)
    aux[me, 0:channels, :] = weight_out_ref[...].astype(jnp.float32)
    aux[me, 16:17, :] = bias_mid_ref[...]

    up_ok = jnp.where(row_place > 0, 1, 0)
    down_ok = jnp.where(row_place < n_row - 1, 1, 0)
    left_ok = jnp.where(col_place > 0, 1, 0)
    right_ok = jnp.where(col_place < n_col - 1, 1, 0)
    links = (1 + up_ok + down_ok) * (1 + left_ok + right_ok)
    pl.semaphore_wait(barrier, links)

    def remote(src, dst, sem, where, arrive=None):
        return pltpu.make_async_remote_copy(
            src_ref=src, dst_ref=dst, send_sem=send_sem.at[sem],
            recv_sem=recv_sem.at[sem if arrive is None else arrive],
            device_id=where, device_id_type=MESH,
        )

    def message(d):
        arrive = BACK[d]
        if d == UP:
            src, dst = center.at[HALO : 2 * HALO], center.at[rows + HALO : rows + 2 * HALO]
        elif d == DOWN:
            src, dst = center.at[rows : rows + HALO], center.at[0:HALO]
        else:
            src, dst = packs.at[8], packs.at[arrive]
        return remote(src, dst, d, target(d), arrive)

    def coarse_message(d):
        if d == LEFT:
            src, dst = coarse_t.at[EDGE : 2 * EDGE], coarse_t.at[EDGE + coarse_here : 2 * EDGE + coarse_here]
        else:
            src, dst = coarse_t.at[coarse_here : EDGE + coarse_here], coarse_t.at[0:EDGE]
        return remote(src, dst, COARSE[d], target(d), COARSE[BACK[d]])

    for d in (LEFT, RIGHT):
        @pl.when(exists(d))
        def _(d=d):
            coarse_message(d).start()
    for d in (UL, UR, DL, DR, UP, DOWN, LEFT, RIGHT):
        @pl.when(exists(d))
        def _(d=d):
            message(d).start()
    send_aux = remote(aux.at[me], aux.at[me], AUX, {"chan": other})
    send_aux.start()
    send_weights = remote(weight_mid_ref, w_mid.at[:, half, :], WEIGHTS, {"chan": other})
    send_weights.start()

    for load in loads[4:]:
        load.wait()

    w_in_t[...] = jnp.zeros_like(w_in_t)
    for i in range(3):
        for j in range(3):
            start = BLOCK * i + GROUP * j
            w_in_t[start : start + GROUP, :] = weight_in_ref[3 * i + j].astype(jnp.float32)
    w_first = jnp.transpose(w_in_t[...]).astype(jnp.bfloat16)[:, 0 : 3 * BLOCK]
    step_here = jnp.full((1, hidden), step_ref[me].astype(jnp.float32), jnp.float32)
    log_noise = rho_power * jnp.log(base_level(step_here))
    cond[...] = column(bias_in_ref[...] + log_noise / 4.0 * weight_noise_ref[...])

    n_coarse = coarse_t.shape[0]
    index = (iota((n_coarse, cols), 0) + (col_place * coarse_here - EDGE)).astype(jnp.float32)
    x_here = iota((n_coarse, cols), 1)
    x_edge = jnp.where(x_here < cols // 2, -2, cols - 1)
    width = n_col * cols
    tables = []
    for x in [x_here + j - 1 for j in range(3)] + [x_edge + j for j in range(3)]:
        x = x + col_place * cols
        weight = blend(x.astype(jnp.float32), index, float(n_col * coarse_here), float(factor))
        tables.append(jnp.where((x >= 0) & (x < width), weight, 0.0))
    table = jnp.concatenate(tables, axis=1)
    y_ext = iota((16, 128), 0) + (row_place * rows - HALO)
    y_valid = (y_ext >= 0) & (y_ext < n_row * rows)
    row_weights = [
        jnp.where(y_valid, blend(y_ext.astype(jnp.float32), float(h), float(coarse_rows), float(factor)), 0.0)
        for h in range(coarse_rows)
    ]

    for d in (LEFT, RIGHT):
        @pl.when(exists(d))
        def _(d=d):
            coarse_message(BACK[d]).wait_recv()
    across = lax.dot_general(
        coarse_t[...], table, (((0,), (0,)), ((), ())),
        precision=lax.Precision.HIGHEST, preferred_element_type=jnp.float32,
    )
    means[...] = across

    def mean_rows(r, which):
        total = None
        for h in range(coarse_rows):
            term = row_weights[h][r : r + 1, :] * means[h * GROUP : (h + 1) * GROUP, which * cols : (which + 1) * cols]
            total = term if total is None else total + term
        return total

    for d in (UP, DOWN, LEFT, RIGHT, UL, UR, DL, DR):
        @pl.when(exists(d))
        def _(d=d):
            message(BACK[d]).wait_recv()

    zeros = jnp.zeros((BLOCK - 3 * GROUP, cols), jnp.float32)
    for r in range(ext):
        if r < HALO:
            from_left, from_right, y = UL, UR, rows - HALO + r
        elif r < rows + HALO:
            from_left, from_right, y = LEFT, RIGHT, r - HALO
        else:
            from_left, from_right, y = DL, DR, r - rows - HALO
        pack_left, pack_right = packs[from_left], packs[from_right]
        near = jnp.where(
            lane < cols // 2, pltpu.roll(pack_left, (-y) % cols, 1), pltpu.roll(pack_right, y, 1)
        )
        far = jnp.where(
            lane < cols // 2, pltpu.roll(pack_left, (-16 - y) % cols, 1), pltpu.roll(pack_right, 16 + y, 1)
        )
        own = center[r]
        shifted = [
            jnp.where(lane == 0, near, pltpu.roll(own, 1, 1)),
            own,
            jnp.where(lane == cols - 1, near, pltpu.roll(own, cols - 1, 1)),
        ]
        edges = [
            jnp.where(lane < cols // 2, far, own),
            near,
            jnp.where(lane < cols // 2, own, far),
        ]
        here = slice(r * cols, (r + 1) * cols)
        xj[:, here] = jnp.concatenate(
            [shifted[j] + mean_rows(r, j) for j in range(3)] + [zeros], axis=0
        ).astype(jnp.bfloat16)
        xe[:, here] = jnp.concatenate(
            [edges[j] + mean_rows(r, 3 + j) for j in range(3)] + [zeros], axis=0
        ).astype(jnp.bfloat16)

    send_aux.wait_recv()
    w_out = jnp.concatenate([aux[0, 0:16], aux[1, 0:16]], axis=1).astype(jnp.bfloat16)
    bias_mid_col[...] = column(jnp.concatenate([aux[0, 16:17], aux[1, 16:17]], axis=1))
    own_weights.wait()
    send_weights.wait_recv()

    wide_lane = iota((hidden, cols), 1)
    side_ok = jnp.where(
        iota((1, cols), 1) < cols // 2, left_ok.astype(jnp.float32), right_ok.astype(jnp.float32)
    )

    def first_section(y):
        def taps(ref):
            return jnp.concatenate(
                [ref[:, (y + i) * cols : (y + i + 2) * cols] for i in range(3)], axis=0
            )
        main = jnp.dot(w_first, taps(xj), preferred_element_type=jnp.float32)
        edge = jnp.dot(w_first, taps(xe), preferred_element_type=jnp.float32)
        for k in range(2):
            part = slice(k * cols, (k + 1) * cols)
            value = silu(main[:, part] + cond[...])
            side = silu(edge[:, part] + cond[...]) * side_ok
            if y + k == 0:
                value, side = value * up_ok.astype(jnp.float32), side * up_ok.astype(jnp.float32)
            if y + k == rows + 1:
                value, side = value * down_ok.astype(jnp.float32), side * down_ok.astype(jnp.float32)
            before = jnp.where(wide_lane == 0, side, pltpu.roll(value, 1, 1))
            after = jnp.where(wide_lane == cols - 1, side, pltpu.roll(value, cols - 1, 1))
            here = slice((y + k) * cols, (y + k + 1) * cols)
            hc[0:hidden, here] = before.astype(jnp.bfloat16)
            hc[hidden : 2 * hidden, here] = value.astype(jnp.bfloat16)
            hc[2 * hidden : 3 * hidden, here] = after.astype(jnp.bfloat16)

    def net_message(p):
        part = net.at[me, 2 * p : 2 * p + 2]
        return remote(part, part, NET + p, {"chan": other})

    def second_section(y):
        total = None
        for i in range(3):
            w = jnp.concatenate([w_mid[3 * i + j] for j in range(3)], axis=1)
            term = jnp.dot(
                w, hc[:, (y + i) * cols : (y + i + 2) * cols], preferred_element_type=jnp.float32
            )
            total = term if total is None else total + term
        wide = jnp.concatenate([bias_mid_col[...]] * 2, axis=1)
        middle = silu(total + wide).astype(jnp.bfloat16)
        out = jnp.dot(w_out, middle, preferred_element_type=jnp.float32)
        for k in range(2):
            net[me, y + k] = out[:, k * cols : (k + 1) * cols]

    first_section(0)
    first_section(2)
    for y in range(0, rows, 2):
        second_section(y)
        if y + 4 < rows + 2:
            first_section(y + 4)
    for p in range(rows // 2):
        net_message(p).start()

    row_local = iota((rows, cols), 0) + row_place * rows
    out_weights = [
        blend(row_local.astype(jnp.float32), float(h), float(coarse_rows), float(factor))
        for h in range(coarse_rows)
    ]
    mean_out = []
    for c in range(channels):
        total = None
        for h in range(coarse_rows):
            at = h * GROUP + channels + c
            term = out_weights[h] * means[at : at + 1, cols : 2 * cols]
            total = term if total is None else total + term
        mean_out.append(total)

    def finish(s):
        step = jnp.full((rows, cols), step_ref[s].astype(jnp.float32), jnp.float32)
        now, later = power7(base_level(step)), power7(base_level(step + 1.0))
        variance = now * now + sigma_data * sigma_data
        scale_now = jnp.sqrt(variance)
        keep = sigma_data * sigma_data / variance * scale_now
        gain = sigma_data * now / scale_now
        shrink = 1.0 / jnp.sqrt(later * later + sigma_data * sigma_data)
        for c in range(channels):
            denoised = keep * latent_ref[s, c] + gain * net[s, :, c, :]
            fine_ref[s, c] = mean_out[c] + denoised
            next_ref[s, c] = (denoised + later * fresh_ref[s, c]) * shrink

    finish(me)
    for p in range(rows // 2):
        net_message(p).wait_recv()
    finish(other)

    for d in range(8):
        @pl.when(exists(d))
        def _(d=d):
            message(d).wait_send()
    for d in (LEFT, RIGHT):
        @pl.when(exists(d))
        def _(d=d):
            coarse_message(d).wait_send()
    send_aux.wait_send()
    send_weights.wait_send()
    for p in range(rows // 2):
        net_message(p).wait_send()


def on_device(
    latent, fresh_noise, step_index, coarse, weight_in, bias_in, weight_noise,
    weight_mid, bias_mid, weight_out,
):
    samples, channels, rows, cols = latent.shape
    coarse_rows, coarse_here = coarse.shape[1], coarse.shape[2]
    hidden = weight_in.shape[1]
    ext = rows + 2 * HALO
    stacked = -(-coarse_rows * GROUP // 128) * 128
    sizes = (lax.axis_size("row"), lax.axis_size("col"), cols // coarse_here)
    f32, bf16 = jnp.float32, jnp.bfloat16
    vmem = pl.BlockSpec(memory_space=pltpu.VMEM)
    specs = [pl.BlockSpec(memory_space=pltpu.HBM)] * 10
    return pl.pallas_call(
        functools.partial(kernel, sizes),
        out_shape=[jax.ShapeDtypeStruct(latent.shape, f32)] * 2,
        in_specs=specs,
        out_specs=[vmem, vmem],
        scratch_shapes=[
            pltpu.VMEM(latent.shape, f32),
            pltpu.VMEM(latent.shape, f32),
            pltpu.SMEM(step_index.shape, jnp.int32),
            pltpu.VMEM(coarse.shape, f32),
            pltpu.VMEM((9, weight_in.shape[2], hidden), bf16),
            pltpu.VMEM((1, hidden), f32),
            pltpu.VMEM((1, hidden), f32),
            pltpu.VMEM((1, hidden // 2), f32),
            pltpu.VMEM(weight_out.shape, bf16),
            pltpu.SemaphoreType.DMA((9,)),
            pltpu.VMEM((ext, GROUP, cols), f32),
            pltpu.VMEM((9, GROUP, cols), f32),
            pltpu.VMEM((coarse_here + 2 * EDGE, stacked), f32),
            pltpu.VMEM((stacked, 128), f32),
            pltpu.VMEM((2, 24, hidden // 2), f32),
            pltpu.VMEM((9, hidden, hidden), bf16),
            pltpu.VMEM((256, hidden), f32),
            pltpu.VMEM((BLOCK, ext * cols), bf16),
            pltpu.VMEM((BLOCK, ext * cols), bf16),
            pltpu.VMEM((3 * hidden, (rows + 2) * cols), bf16),
            pltpu.VMEM((samples, rows, 16, cols), f32),
            pltpu.VMEM((stacked, 6 * cols), f32),
            pltpu.VMEM((hidden, cols), f32),
            pltpu.VMEM((hidden, cols), f32),
            pltpu.SemaphoreType.DMA((12 + rows // 2,)),
            pltpu.SemaphoreType.DMA((12 + rows // 2,)),
            pltpu.SemaphoreType.DMA,
        ],
        compiler_params=pltpu.CompilerParams(
            collective_id=0, has_side_effects=True, vmem_limit_bytes=64 * 1024 * 1024
        ),
        name="denoise_step",
    )(
        latent, fresh_noise, step_index, coarse, jnp.transpose(weight_in, (0, 2, 1)), bias_in.reshape(1, hidden),
        weight_noise.reshape(1, hidden), weight_mid, bias_mid.reshape(1, hidden // 2), weight_out,
    )


def solution(mesh):
    in_specs = (
        P("ens", None, "row", "col"),
        P("ens", None, "row", "col"),
        P("ens"),
        P("ens", None, "col"),
        P(),
        P(),
        P(),
        P(None, "chan", None),
        P("chan"),
        P(None, "chan"),
    )
    out_specs = (P("ens", None, "row", "col"), P("ens", None, "row", "col"))
    return jax.shard_map(
        on_device, mesh=mesh, in_specs=in_specs, out_specs=out_specs, check_vma=False
    )
```

```python
import functools

import jax
import jax.numpy as jnp
from jax import lax
from jax.experimental import pallas as pl
from jax.experimental.pallas import tpu as pltpu
from jax.sharding import PartitionSpec as P

STEPS = 18
sigma_data = 0.5
sigma_high = 80.0
sigma_low = 0.002
rho_power = 7.0
top_root = sigma_high ** (1.0 / rho_power)
bottom_root = sigma_low ** (1.0 / rho_power)

MESH = pl.DeviceIdType.MESH
UP, DOWN, LEFT, RIGHT, UL, UR, DL, DR = range(8)
STEP = {
    UP: (-1, 0), DOWN: (1, 0), LEFT: (0, -1), RIGHT: (0, 1),
    UL: (-1, -1), UR: (-1, 1), DL: (1, -1), DR: (1, 1),
}
BACK = {UP: DOWN, DOWN: UP, LEFT: RIGHT, RIGHT: LEFT, UL: DR, DR: UL, UR: DL, DL: UR}
COARSE = {LEFT: 8, RIGHT: 9}
WEIGHTS, AUX, NET = 10, 11, 12
HALO = 2
GROUP = 24
BLOCK = 80
EDGE = 8


def silu(v):
    half = 0.5 * v
    return half * (1.0 + jnp.tanh(half))


def iota(shape, dim):
    return lax.broadcasted_iota(jnp.int32, shape, dim)


def blend(position, index, count, factor):
    u = (position + 0.5) / factor - 0.5
    cell = jnp.floor(u)
    fraction = jnp.where(u < 0.0, 0.0, u - cell)
    low = jnp.maximum(cell, 0.0)
    high = jnp.minimum(jnp.maximum(cell + 1.0, 0.0), count - 1.0)
    low_hit = jnp.where(low == index, 1.0 - fraction, 0.0)
    high_hit = jnp.where(high == index, fraction, 0.0)
    return low_hit + high_hit


def base_level(step):
    return top_root + step / (STEPS - 1) * (bottom_root - top_root)


def power7(b):
    b2 = b * b
    return b2 * b2 * b2 * b


def column(row_vector):
    n = row_vector.shape[1]
    parts = [
        jnp.transpose(jnp.broadcast_to(row_vector[:, a : a + 128], (128, 128)))
        for a in range(0, n, 128)
    ]
    return parts[0] if len(parts) == 1 else jnp.concatenate(parts, axis=0)


def kernel(
    sizes,
    latent_hbm, fresh_hbm, step_hbm, coarse_hbm, weight_in_hbm, bias_in_hbm, weight_noise_hbm,
    weight_mid_ref, bias_mid_hbm, weight_out_hbm,
    denoised_hbm, mean_hbm, noise_hbm, shrink_hbm,
    denoised_ref, mean_ref, noise_ref, shrink_ref, store_sem,
    latent_ref, fresh_ref, step_ref, coarse_ref, weight_in_ref, bias_in_ref, weight_noise_ref,
    bias_mid_ref, weight_out_ref, load_sem,
    center, packs, coarse_t, coarse_st, aux, w_mid, w_in_t, xj, xe, hc, net, means, cond, bias_mid_col,
    send_sem, recv_sem, own_sem,
):
    n_row, n_col, factor = sizes
    samples, channels, rows, cols = latent_ref.shape
    coarse_rows, coarse_here = coarse_ref.shape[1], coarse_ref.shape[2]
    hidden = weight_in_ref.shape[2]
    half_hidden = hidden // 2
    ext = rows + 2 * HALO
    row_place, col_place = lax.axis_index("row"), lax.axis_index("col")
    me = lax.axis_index("chan")
    other = 1 - me

    def exists(d):
        dr, dc = STEP[d]
        conds = []
        if dr < 0:
            conds.append(row_place > 0)
        if dr > 0:
            conds.append(row_place < n_row - 1)
        if dc < 0:
            conds.append(col_place > 0)
        if dc > 0:
            conds.append(col_place < n_col - 1)
        return conds[0] if len(conds) == 1 else jnp.logical_and(*conds)

    def target(d):
        return {"row": row_place + STEP[d][0], "col": col_place + STEP[d][1]}

    loads = [
        pltpu.make_async_copy(src, dst, load_sem.at[n])
        for n, (src, dst) in enumerate((
            (latent_hbm, latent_ref), (coarse_hbm, coarse_ref), (weight_out_hbm, weight_out_ref),
            (bias_mid_hbm, bias_mid_ref), (weight_in_hbm, weight_in_ref), (step_hbm, step_ref),
            (bias_in_hbm, bias_in_ref), (weight_noise_hbm, weight_noise_ref), (fresh_hbm, fresh_ref),
        ))
    ]
    for load in loads:
        load.start()

    center[...] = jnp.zeros_like(center)
    packs[...] = jnp.zeros_like(packs)
    coarse_t[...] = jnp.zeros_like(coarse_t)

    barrier = pltpu.get_barrier_semaphore()
    pl.semaphore_signal(barrier, inc=1, device_id={"chan": other}, device_id_type=MESH)
    for d in range(8):
        @pl.when(exists(d))
        def _(d=d):
            pl.semaphore_signal(barrier, inc=1, device_id=target(d), device_id_type=MESH)

    half = pl.ds(pl.multiple_of(me * half_hidden, half_hidden), half_hidden)
    own_weights = pltpu.make_async_copy(weight_mid_ref, w_mid.at[:, half, :], own_sem)
    own_weights.start()

    up_ok = jnp.where(row_place > 0, 1, 0)
    down_ok = jnp.where(row_place < n_row - 1, 1, 0)
    left_ok = jnp.where(col_place > 0, 1, 0)
    right_ok = jnp.where(col_place < n_col - 1, 1, 0)
    pl.semaphore_wait(barrier, (1 + up_ok + down_ok) * (1 + left_ok + right_ok))

    def remote(src, dst, sem, where, arrive=None):
        return pltpu.make_async_remote_copy(
            src_ref=src, dst_ref=dst, send_sem=send_sem.at[sem],
            recv_sem=recv_sem.at[sem if arrive is None else arrive],
            device_id=where, device_id_type=MESH,
        )

    def message(d):
        arrive = BACK[d]
        if d == UP:
            src, dst = center.at[HALO : 2 * HALO], center.at[rows + HALO : rows + 2 * HALO]
        elif d == DOWN:
            src, dst = center.at[rows : rows + HALO], center.at[0:HALO]
        else:
            src, dst = packs.at[8], packs.at[arrive]
        return remote(src, dst, d, target(d), arrive)

    def coarse_message(d):
        if d == LEFT:
            src, dst = coarse_t.at[EDGE : 2 * EDGE], coarse_t.at[EDGE + coarse_here : 2 * EDGE + coarse_here]
        else:
            src, dst = coarse_t.at[coarse_here : EDGE + coarse_here], coarse_t.at[0:EDGE]
        return remote(src, dst, COARSE[d], target(d), COARSE[BACK[d]])

    def each(directions, act):
        for d in directions:
            @pl.when(exists(d))
            def _(d=d):
                act(d)

    send_weights = remote(weight_mid_ref, w_mid.at[:, half, :], WEIGHTS, {"chan": other})
    send_weights.start()

    for load in loads[0:2]:
        load.wait()
    lane = iota((GROUP, cols), 1)
    for y in range(rows):
        center[HALO + y, 0:channels, :] = latent_ref[me, :, y, :]
    each((UP, DOWN), lambda d: message(d).start())
    pack = jnp.zeros((GROUP, cols), jnp.float32)
    for y in range(rows):
        v = center[HALO + y]
        for source, place in ((cols - 1, y), (cols - 2, 16 + y), (0, cols - 1 - y), (1, cols - 17 - y)):
            pack = jnp.where(lane == place, pltpu.roll(v, (place - source) % cols, 1), pack)
    packs[8] = pack
    coarse_st[...] = jnp.zeros_like(coarse_st)
    for h in range(coarse_rows):
        start = h * GROUP + channels
        coarse_st[start : start + channels, 0:coarse_here] = coarse_ref[:, h, :]
    turned = jnp.transpose(coarse_st[...])
    coarse_t[EDGE : EDGE + coarse_here, :] = turned[0:coarse_here, :]
    each((UL, UR, DL, DR, LEFT, RIGHT), lambda d: message(d).start())
    each((LEFT, RIGHT), lambda d: coarse_message(d).start())
    for load in loads[2:4]:
        load.wait()
    aux[me] = jnp.zeros(aux.shape[1:], jnp.float32)
    aux[me, 0:channels, :] = weight_out_ref[...].astype(jnp.float32)
    aux[me, 16:17, :] = bias_mid_ref[...]
    send_aux = remote(aux.at[me], aux.at[me], AUX, {"chan": other})
    send_aux.start()
    for load in loads[4:]:
        load.wait()

    w_in_t[...] = jnp.zeros_like(w_in_t)
    for i in range(3):
        for j in range(3):
            start = BLOCK * i + GROUP * j
            w_in_t[start : start + GROUP, :] = weight_in_ref[3 * i + j].astype(jnp.float32)
    w_first = jnp.transpose(w_in_t[...]).astype(jnp.bfloat16)[:, 0 : 3 * BLOCK]
    step_here = jnp.full((1, hidden), step_ref[me].astype(jnp.float32), jnp.float32)
    log_noise = rho_power * jnp.log(base_level(step_here))
    cond[...] = column(bias_in_ref[...] + log_noise / 4.0 * weight_noise_ref[...])

    n_coarse = coarse_t.shape[0]
    index = (iota((n_coarse, cols), 0) + (col_place * coarse_here - EDGE)).astype(jnp.float32)
    x_here = iota((n_coarse, cols), 1)
    x_edge = jnp.where(x_here < cols // 2, -2, cols - 1)
    width = n_col * cols
    tables = []
    for x in [x_here + j - 1 for j in range(3)] + [x_edge + j for j in range(3)]:
        x = x + col_place * cols
        weight = blend(x.astype(jnp.float32), index, float(n_col * coarse_here), float(factor))
        tables.append(jnp.where((x >= 0) & (x < width), weight, 0.0))
    table = jnp.concatenate(tables, axis=1)
    y_ext = iota((16, 128), 0) + (row_place * rows - HALO)
    y_valid = (y_ext >= 0) & (y_ext < n_row * rows)
    row_weights = [
        jnp.where(y_valid, blend(y_ext.astype(jnp.float32), float(h), float(coarse_rows), float(factor)), 0.0)
        for h in range(coarse_rows)
    ]

    each((LEFT, RIGHT), lambda d: coarse_message(BACK[d]).wait_recv())
    across = lax.dot_general(
        coarse_t[...], table, (((0,), (0,)), ((), ())),
        precision=lax.Precision.HIGHEST, preferred_element_type=jnp.float32,
    )
    means[...] = across

    def mean_rows(r, which):
        total = None
        for h in range(coarse_rows):
            term = row_weights[h][r : r + 1, :] * means[h * GROUP : (h + 1) * GROUP, which * cols : (which + 1) * cols]
            total = term if total is None else total + term
        return total

    row_local = iota((rows, cols), 0) + row_place * rows
    out_weights = [
        blend(row_local.astype(jnp.float32), float(h), float(coarse_rows), float(factor))
        for h in range(coarse_rows)
    ]
    for c in range(channels):
        total = None
        for h in range(coarse_rows):
            at = h * GROUP + channels + c
            term = out_weights[h] * means[at : at + 1, cols : 2 * cols]
            total = term if total is None else total + term
        mean_ref[c] = total

    def levels(s):
        step = jnp.full((rows, cols), step_ref[s].astype(jnp.float32), jnp.float32)
        return power7(base_level(step)), power7(base_level(step + 1.0))

    for s in range(samples):
        now, later = levels(s)
        shrink = 1.0 / jnp.sqrt(later * later + sigma_data * sigma_data)
        shrink_ref[s, 0] = shrink
        for c in range(channels):
            noise_ref[s, c] = later * fresh_ref[s, c] * shrink
    stores = [
        pltpu.make_async_copy(src, dst, store_sem.at[n])
        for n, (src, dst) in enumerate((
            (mean_ref, mean_hbm), (noise_ref, noise_hbm), (shrink_ref, shrink_hbm),
            (denoised_ref.at[me], denoised_hbm.at[me]), (denoised_ref.at[other], denoised_hbm.at[other]),
        ))
    ]
    for store in stores[0:3]:
        store.start()

    zeros = jnp.zeros((BLOCK - 3 * GROUP, cols), jnp.float32)

    def prepare(r):
        if r < HALO:
            from_left, from_right, y = UL, UR, rows - HALO + r
        elif r < rows + HALO:
            from_left, from_right, y = LEFT, RIGHT, r - HALO
        else:
            from_left, from_right, y = DL, DR, r - rows - HALO
        pack_left, pack_right = packs[from_left], packs[from_right]
        near = jnp.where(
            lane < cols // 2, pltpu.roll(pack_left, (-y) % cols, 1), pltpu.roll(pack_right, y, 1)
        )
        far = jnp.where(
            lane < cols // 2, pltpu.roll(pack_left, (-16 - y) % cols, 1), pltpu.roll(pack_right, 16 + y, 1)
        )
        own = center[r]
        shifted = [
            jnp.where(lane == 0, near, pltpu.roll(own, 1, 1)),
            own,
            jnp.where(lane == cols - 1, near, pltpu.roll(own, cols - 1, 1)),
        ]
        edges = [
            jnp.where(lane < cols // 2, far, own),
            near,
            jnp.where(lane < cols // 2, own, far),
        ]
        here = slice(r * cols, (r + 1) * cols)
        xj[:, here] = jnp.concatenate(
            [shifted[j] + mean_rows(r, j) for j in range(3)] + [zeros], axis=0
        ).astype(jnp.bfloat16)
        xe[:, here] = jnp.concatenate(
            [edges[j] + mean_rows(r, 3 + j) for j in range(3)] + [zeros], axis=0
        ).astype(jnp.bfloat16)

    wide_lane = iota((hidden, cols), 1)
    side_ok = jnp.where(
        iota((1, cols), 1) < cols // 2, left_ok.astype(jnp.float32), right_ok.astype(jnp.float32)
    )

    def first_section(y):
        def taps(ref):
            return jnp.concatenate(
                [ref[:, (y + i) * cols : (y + i + 2) * cols] for i in range(3)], axis=0
            )
        main = jnp.dot(w_first, taps(xj), preferred_element_type=jnp.float32)
        edge = jnp.dot(w_first, taps(xe), preferred_element_type=jnp.float32)
        for k in range(2):
            part = slice(k * cols, (k + 1) * cols)
            value = silu(main[:, part] + cond[...])
            side = silu(edge[:, part] + cond[...]) * side_ok
            if y + k == 0:
                value, side = value * up_ok.astype(jnp.float32), side * up_ok.astype(jnp.float32)
            if y + k == rows + 1:
                value, side = value * down_ok.astype(jnp.float32), side * down_ok.astype(jnp.float32)
            before = jnp.where(wide_lane == 0, side, pltpu.roll(value, 1, 1))
            after = jnp.where(wide_lane == cols - 1, side, pltpu.roll(value, cols - 1, 1))
            here = slice((y + k) * cols, (y + k + 1) * cols)
            hc[0:hidden, here] = before.astype(jnp.bfloat16)
            hc[hidden : 2 * hidden, here] = value.astype(jnp.bfloat16)
            hc[2 * hidden : 3 * hidden, here] = after.astype(jnp.bfloat16)

    def net_message(p):
        part = net.at[me, 2 * p : 2 * p + 2]
        return remote(part, part, NET + p, {"chan": other})

    def second_section(y):
        total = None
        for i in range(3):
            w = jnp.concatenate([w_mid[3 * i + j] for j in range(3)], axis=1)
            term = jnp.dot(
                w, hc[:, (y + i) * cols : (y + i + 2) * cols], preferred_element_type=jnp.float32
            )
            total = term if total is None else total + term
        wide = jnp.concatenate([bias_mid_col[...]] * 2, axis=1)
        middle = silu(total + wide).astype(jnp.bfloat16)
        out = jnp.dot(w_out, middle, preferred_element_type=jnp.float32)
        for k in range(2):
            net[me, y + k] = out[:, k * cols : (k + 1) * cols]

    each((LEFT, RIGHT), lambda d: message(BACK[d]).wait_recv())
    for r in range(HALO, rows + HALO):
        prepare(r)
    send_aux.wait_recv()
    w_out = jnp.concatenate([aux[0, 0:16], aux[1, 0:16]], axis=1).astype(jnp.bfloat16)
    bias_mid_col[...] = column(jnp.concatenate([aux[0, 16:17], aux[1, 16:17]], axis=1))
    own_weights.wait()
    send_weights.wait_recv()

    first_section(2)
    for y in range(2, rows - 2, 2):
        first_section(y + 2)
        second_section(y)
    for p in range(1, rows // 2 - 1):
        net_message(p).start()
    each((UP, DOWN, UL, UR, DL, DR), lambda d: message(BACK[d]).wait_recv())
    for r in [*range(HALO), *range(rows + HALO, ext)]:
        prepare(r)
    first_section(0)
    first_section(rows)
    second_section(0)
    second_section(rows - 2)
    for p in (0, rows // 2 - 1):
        net_message(p).start()

    def finish(s):
        now, later = levels(s)
        variance = now * now + sigma_data * sigma_data
        scale_now = jnp.sqrt(variance)
        keep = sigma_data * sigma_data / variance * scale_now
        gain = sigma_data * now / scale_now
        for c in range(channels):
            denoised_ref[s, c] = keep * latent_ref[s, c] + gain * net[s, :, c, :]

    finish(me)
    stores[3].start()
    for p in range(rows // 2):
        net_message(p).wait_recv()
    finish(other)
    stores[4].start()

    for d in range(8):
        @pl.when(exists(d))
        def _(d=d):
            message(d).wait_send()
    for d in (LEFT, RIGHT):
        @pl.when(exists(d))
        def _(d=d):
            coarse_message(d).wait_send()
    send_aux.wait_send()
    send_weights.wait_send()
    for p in range(rows // 2):
        net_message(p).wait_send()
    for store in stores:
        store.wait()


def on_device(
    latent, fresh_noise, step_index, coarse, weight_in, bias_in, weight_noise,
    weight_mid, bias_mid, weight_out,
):
    samples, channels, rows, cols = latent.shape
    coarse_rows, coarse_here = coarse.shape[1], coarse.shape[2]
    hidden = weight_in.shape[1]
    ext = rows + 2 * HALO
    stacked = -(-coarse_rows * GROUP // 128) * 128
    sizes = (lax.axis_size("row"), lax.axis_size("col"), cols // coarse_here)
    f32, bf16 = jnp.float32, jnp.bfloat16
    specs = [pl.BlockSpec(memory_space=pltpu.HBM)] * 10
    out_shapes = [latent.shape, latent.shape[1:], latent.shape, (samples, 1, rows, cols)]
    denoised, mean, noise, shrink = pl.pallas_call(
        functools.partial(kernel, sizes),
        out_shape=[jax.ShapeDtypeStruct(shape, f32) for shape in out_shapes],
        in_specs=specs,
        out_specs=[pl.BlockSpec(memory_space=pltpu.HBM)] * 4,
        scratch_shapes=[
            *[pltpu.VMEM(shape, f32) for shape in out_shapes],
            pltpu.SemaphoreType.DMA((5,)),
            pltpu.VMEM(latent.shape, f32),
            pltpu.VMEM(latent.shape, f32),
            pltpu.SMEM(step_index.shape, jnp.int32),
            pltpu.VMEM(coarse.shape, f32),
            pltpu.VMEM((9, weight_in.shape[2], hidden), bf16),
            pltpu.VMEM((1, hidden), f32),
            pltpu.VMEM((1, hidden), f32),
            pltpu.VMEM((1, hidden // 2), f32),
            pltpu.VMEM(weight_out.shape, bf16),
            pltpu.SemaphoreType.DMA((9,)),
            pltpu.VMEM((ext, GROUP, cols), f32),
            pltpu.VMEM((9, GROUP, cols), f32),
            pltpu.VMEM((coarse_here + 2 * EDGE, stacked), f32),
            pltpu.VMEM((stacked, 128), f32),
            pltpu.VMEM((2, 24, hidden // 2), f32),
            pltpu.VMEM((9, hidden, hidden), bf16),
            pltpu.VMEM((256, hidden), f32),
            pltpu.VMEM((BLOCK, ext * cols), bf16),
            pltpu.VMEM((BLOCK, ext * cols), bf16),
            pltpu.VMEM((3 * hidden, (rows + 2) * cols), bf16),
            pltpu.VMEM((samples, rows, 16, cols), f32),
            pltpu.VMEM((stacked, 6 * cols), f32),
            pltpu.VMEM((hidden, cols), f32),
            pltpu.VMEM((hidden, cols), f32),
            pltpu.SemaphoreType.DMA((12 + rows // 2,)),
            pltpu.SemaphoreType.DMA((12 + rows // 2,)),
            pltpu.SemaphoreType.DMA,
        ],
        compiler_params=pltpu.CompilerParams(
            collective_id=0, has_side_effects=True, vmem_limit_bytes=64 * 1024 * 1024
        ),
        name="denoise_step",
    )(
        latent, fresh_noise, step_index, coarse, jnp.transpose(weight_in, (0, 2, 1)), bias_in.reshape(1, hidden),
        weight_noise.reshape(1, hidden), weight_mid, bias_mid.reshape(1, hidden // 2), weight_out,
    )
    return mean[None] + denoised, denoised * shrink + noise


def solution(mesh):
    in_specs = (
        P("ens", None, "row", "col"),
        P("ens", None, "row", "col"),
        P("ens"),
        P("ens", None, "col"),
        P(),
        P(),
        P(),
        P(None, "chan", None),
        P("chan"),
        P(None, "chan"),
    )
    out_specs = (P("ens", None, "row", "col"), P("ens", None, "row", "col"))
    return jax.shard_map(
        on_device, mesh=mesh, in_specs=in_specs, out_specs=out_specs, check_vma=False
    )
```

```python
import functools

import jax
import jax.numpy as jnp
from jax import lax
from jax.experimental import pallas as pl
from jax.experimental.pallas import tpu as pltpu
from jax.sharding import PartitionSpec as P

STEPS = 18
sigma_data = 0.5
sigma_high = 80.0
sigma_low = 0.002
rho_power = 7.0
top_root = sigma_high ** (1.0 / rho_power)
bottom_root = sigma_low ** (1.0 / rho_power)

MESH = pl.DeviceIdType.MESH
UP, DOWN, LEFT, RIGHT, UL, UR, DL, DR = range(8)
STEP = {
    UP: (-1, 0), DOWN: (1, 0), LEFT: (0, -1), RIGHT: (0, 1),
    UL: (-1, -1), UR: (-1, 1), DL: (1, -1), DR: (1, 1),
}
BACK = {UP: DOWN, DOWN: UP, LEFT: RIGHT, RIGHT: LEFT, UL: DR, DR: UL, UR: DL, DL: UR}
COARSE = {LEFT: 8, RIGHT: 9}
WEIGHTS, AUX, NET = 10, 11, 12
HALO = 2
GROUP = 24
BLOCK = 80
EDGE = 8


def silu(v):
    half = 0.5 * v
    return half * (1.0 + jnp.tanh(half))


def iota(shape, dim):
    return lax.broadcasted_iota(jnp.int32, shape, dim)


def blend(position, index, count, factor):
    u = (position + 0.5) / factor - 0.5
    cell = jnp.floor(u)
    fraction = jnp.where(u < 0.0, 0.0, u - cell)
    low = jnp.maximum(cell, 0.0)
    high = jnp.minimum(jnp.maximum(cell + 1.0, 0.0), count - 1.0)
    low_hit = jnp.where(low == index, 1.0 - fraction, 0.0)
    high_hit = jnp.where(high == index, fraction, 0.0)
    return low_hit + high_hit


def base_level(step):
    return top_root + step / (STEPS - 1) * (bottom_root - top_root)


def power7(b):
    b2 = b * b
    return b2 * b2 * b2 * b


def column(row_vector):
    n = row_vector.shape[1]
    parts = [
        jnp.transpose(jnp.broadcast_to(row_vector[:, a : a + 128], (128, 128)))
        for a in range(0, n, 128)
    ]
    return parts[0] if len(parts) == 1 else jnp.concatenate(parts, axis=0)


def kernel(
    sizes,
    latent_hbm, fresh_hbm, step_hbm, coarse_hbm, weight_in_hbm, bias_in_hbm, weight_noise_hbm,
    weight_mid_ref, bias_mid_hbm, weight_out_hbm,
    denoised_hbm, mean_hbm, noise_hbm, shrink_hbm,
    denoised_ref, mean_ref, noise_ref, shrink_ref, store_sem,
    latent_ref, fresh_ref, step_ref, coarse_ref, weight_in_ref, bias_in_ref, weight_noise_ref,
    bias_mid_ref, weight_out_ref, load_sem,
    center, packs, coarse_t, coarse_st, aux, w_mid, w_in_t, xj, xe, hc, net, means, cond, bias_mid_col,
    send_sem, recv_sem, own_sem,
):
    n_row, n_col, factor = sizes
    samples, channels, rows, cols = latent_ref.shape
    coarse_rows, coarse_here = coarse_ref.shape[1], coarse_ref.shape[2]
    hidden = weight_in_ref.shape[2]
    half_hidden = hidden // 2
    ext = rows + 2 * HALO
    row_place, col_place = lax.axis_index("row"), lax.axis_index("col")
    me = lax.axis_index("chan")
    other = 1 - me

    def exists(d):
        dr, dc = STEP[d]
        conds = []
        if dr < 0:
            conds.append(row_place > 0)
        if dr > 0:
            conds.append(row_place < n_row - 1)
        if dc < 0:
            conds.append(col_place > 0)
        if dc > 0:
            conds.append(col_place < n_col - 1)
        return conds[0] if len(conds) == 1 else jnp.logical_and(*conds)

    def target(d):
        return {"row": row_place + STEP[d][0], "col": col_place + STEP[d][1]}

    loads = [
        pltpu.make_async_copy(src, dst, load_sem.at[n])
        for n, (src, dst) in enumerate((
            (latent_hbm, latent_ref), (coarse_hbm, coarse_ref), (weight_out_hbm, weight_out_ref),
            (bias_mid_hbm, bias_mid_ref), (weight_in_hbm, weight_in_ref), (step_hbm, step_ref),
            (bias_in_hbm, bias_in_ref), (weight_noise_hbm, weight_noise_ref), (fresh_hbm, fresh_ref),
        ))
    ]
    for load in loads:
        load.start()

    center[...] = jnp.zeros_like(center)
    packs[...] = jnp.zeros_like(packs)
    coarse_t[...] = jnp.zeros_like(coarse_t)

    barrier = pltpu.get_barrier_semaphore()
    pl.semaphore_signal(barrier, inc=1, device_id={"chan": other}, device_id_type=MESH)
    for d in range(8):
        @pl.when(exists(d))
        def _(d=d):
            pl.semaphore_signal(barrier, inc=1, device_id=target(d), device_id_type=MESH)

    half = pl.ds(pl.multiple_of(me * half_hidden, half_hidden), half_hidden)
    own_weights = pltpu.make_async_copy(weight_mid_ref, w_mid.at[:, half, :], own_sem)
    own_weights.start()

    up_ok = jnp.where(row_place > 0, 1, 0)
    down_ok = jnp.where(row_place < n_row - 1, 1, 0)
    left_ok = jnp.where(col_place > 0, 1, 0)
    right_ok = jnp.where(col_place < n_col - 1, 1, 0)
    pl.semaphore_wait(barrier, (1 + up_ok + down_ok) * (1 + left_ok + right_ok))

    def remote(src, dst, sem, where, arrive=None):
        return pltpu.make_async_remote_copy(
            src_ref=src, dst_ref=dst, send_sem=send_sem.at[sem],
            recv_sem=recv_sem.at[sem if arrive is None else arrive],
            device_id=where, device_id_type=MESH,
        )

    def message(d):
        arrive = BACK[d]
        if d == UP:
            src, dst = center.at[HALO : 2 * HALO], center.at[rows + HALO : rows + 2 * HALO]
        elif d == DOWN:
            src, dst = center.at[rows : rows + HALO], center.at[0:HALO]
        else:
            src, dst = packs.at[8], packs.at[arrive]
        return remote(src, dst, d, target(d), arrive)

    def coarse_message(d):
        if d == LEFT:
            src, dst = coarse_t.at[EDGE : 2 * EDGE], coarse_t.at[EDGE + coarse_here : 2 * EDGE + coarse_here]
        else:
            src, dst = coarse_t.at[coarse_here : EDGE + coarse_here], coarse_t.at[0:EDGE]
        return remote(src, dst, COARSE[d], target(d), COARSE[BACK[d]])

    def each(directions, act):
        for d in directions:
            @pl.when(exists(d))
            def _(d=d):
                act(d)

    send_weights = remote(weight_mid_ref, w_mid.at[:, half, :], WEIGHTS, {"chan": other})
    send_weights.start()

    for load in loads[0:2]:
        load.wait()
    lane = iota((GROUP, cols), 1)
    for y in range(rows):
        center[HALO + y, 0:channels, :] = latent_ref[me, :, y, :]
    each((UP, DOWN), lambda d: message(d).start())
    pack = jnp.zeros((GROUP, cols), jnp.float32)
    for y in range(rows):
        v = center[HALO + y]
        for source, place in ((cols - 1, y), (cols - 2, 16 + y), (0, cols - 1 - y), (1, cols - 17 - y)):
            pack = jnp.where(lane == place, pltpu.roll(v, (place - source) % cols, 1), pack)
    packs[8] = pack
    coarse_st[...] = jnp.zeros_like(coarse_st)
    for h in range(coarse_rows):
        start = h * GROUP + channels
        coarse_st[start : start + channels, 0:coarse_here] = coarse_ref[:, h, :]
    turned = jnp.transpose(coarse_st[...])
    coarse_t[EDGE : EDGE + coarse_here, :] = turned[0:coarse_here, :]
    each((UL, UR, DL, DR, LEFT, RIGHT), lambda d: message(d).start())
    each((LEFT, RIGHT), lambda d: coarse_message(d).start())
    for load in loads[2:4]:
        load.wait()
    aux[me] = jnp.zeros(aux.shape[1:], jnp.float32)
    aux[me, 0:channels, :] = weight_out_ref[...].astype(jnp.float32)
    aux[me, 16:17, :] = bias_mid_ref[...]
    send_aux = remote(aux.at[me], aux.at[me], AUX, {"chan": other})
    send_aux.start()
    for load in loads[4:]:
        load.wait()

    w_in_t[...] = jnp.zeros_like(w_in_t)
    for i in range(3):
        for j in range(3):
            start = BLOCK * i + GROUP * j
            w_in_t[start : start + GROUP, :] = weight_in_ref[3 * i + j].astype(jnp.float32)
    w_first = jnp.transpose(w_in_t[...]).astype(jnp.bfloat16)[:, 0 : 3 * BLOCK]
    step_here = jnp.full((1, hidden), step_ref[me].astype(jnp.float32), jnp.float32)
    log_noise = rho_power * jnp.log(base_level(step_here))
    cond[...] = column(bias_in_ref[...] + log_noise / 4.0 * weight_noise_ref[...])

    n_coarse = coarse_t.shape[0]
    index = (iota((n_coarse, cols), 0) + (col_place * coarse_here - EDGE)).astype(jnp.float32)
    x_here = iota((n_coarse, cols), 1)
    x_edge = jnp.where(x_here < cols // 2, -2, cols - 1)
    width = n_col * cols
    tables = []
    for x in [x_here + j - 1 for j in range(3)] + [x_edge + j for j in range(3)]:
        x = x + col_place * cols
        weight = blend(x.astype(jnp.float32), index, float(n_col * coarse_here), float(factor))
        tables.append(jnp.where((x >= 0) & (x < width), weight, 0.0))
    table = jnp.concatenate(tables, axis=1)
    y_ext = iota((16, 128), 0) + (row_place * rows - HALO)
    y_valid = (y_ext >= 0) & (y_ext < n_row * rows)
    row_weights = [
        jnp.where(y_valid, blend(y_ext.astype(jnp.float32), float(h), float(coarse_rows), float(factor)), 0.0)
        for h in range(coarse_rows)
    ]

    each((LEFT, RIGHT), lambda d: coarse_message(BACK[d]).wait_recv())
    across = lax.dot_general(
        coarse_t[...], table, (((0,), (0,)), ((), ())),
        precision=lax.Precision.HIGHEST, preferred_element_type=jnp.float32,
    )
    means[...] = across

    def mean_rows(r, which):
        total = None
        for h in range(coarse_rows):
            term = row_weights[h][r : r + 1, :] * means[h * GROUP : (h + 1) * GROUP, which * cols : (which + 1) * cols]
            total = term if total is None else total + term
        return total

    row_local = iota((rows, cols), 0) + row_place * rows
    out_weights = [
        blend(row_local.astype(jnp.float32), float(h), float(coarse_rows), float(factor))
        for h in range(coarse_rows)
    ]
    for c in range(channels):
        total = None
        for h in range(coarse_rows):
            at = h * GROUP + channels + c
            term = out_weights[h] * means[at : at + 1, cols : 2 * cols]
            total = term if total is None else total + term
        mean_ref[c] = total

    def levels(s):
        step = jnp.full((rows, cols), step_ref[s].astype(jnp.float32), jnp.float32)
        return power7(base_level(step)), power7(base_level(step + 1.0))

    for s in range(samples):
        now, later = levels(s)
        shrink = 1.0 / jnp.sqrt(later * later + sigma_data * sigma_data)
        for c in range(channels):
            noise_ref[s, c] = later * fresh_ref[s, c] * shrink
            shrink_ref[s, c] = shrink
    stores = [
        pltpu.make_async_copy(src, dst, store_sem.at[n])
        for n, (src, dst) in enumerate((
            (mean_ref, mean_hbm), (noise_ref, noise_hbm), (shrink_ref, shrink_hbm),
            (denoised_ref.at[me], denoised_hbm.at[me]), (denoised_ref.at[other], denoised_hbm.at[other]),
        ))
    ]
    for store in stores[0:3]:
        store.start()

    zeros = jnp.zeros((BLOCK - 3 * GROUP, cols), jnp.float32)

    def prepare(r):
        if r < HALO:
            from_left, from_right, y = UL, UR, rows - HALO + r
        elif r < rows + HALO:
            from_left, from_right, y = LEFT, RIGHT, r - HALO
        else:
            from_left, from_right, y = DL, DR, r - rows - HALO
        pack_left, pack_right = packs[from_left], packs[from_right]
        near = jnp.where(
            lane < cols // 2, pltpu.roll(pack_left, (-y) % cols, 1), pltpu.roll(pack_right, y, 1)
        )
        far = jnp.where(
            lane < cols // 2, pltpu.roll(pack_left, (-16 - y) % cols, 1), pltpu.roll(pack_right, 16 + y, 1)
        )
        own = center[r]
        shifted = [
            jnp.where(lane == 0, near, pltpu.roll(own, 1, 1)),
            own,
            jnp.where(lane == cols - 1, near, pltpu.roll(own, cols - 1, 1)),
        ]
        edges = [
            jnp.where(lane < cols // 2, far, own),
            near,
            jnp.where(lane < cols // 2, own, far),
        ]
        here = slice(r * cols, (r + 1) * cols)
        xj[:, here] = jnp.concatenate(
            [shifted[j] + mean_rows(r, j) for j in range(3)] + [zeros], axis=0
        ).astype(jnp.bfloat16)
        xe[:, here] = jnp.concatenate(
            [edges[j] + mean_rows(r, 3 + j) for j in range(3)] + [zeros], axis=0
        ).astype(jnp.bfloat16)

    wide_lane = iota((hidden, cols), 1)
    side_ok = jnp.where(
        iota((1, cols), 1) < cols // 2, left_ok.astype(jnp.float32), right_ok.astype(jnp.float32)
    )

    def first_section(y):
        def taps(ref):
            return jnp.concatenate(
                [ref[:, (y + i) * cols : (y + i + 2) * cols] for i in range(3)], axis=0
            )
        main = jnp.dot(w_first, taps(xj), preferred_element_type=jnp.float32)
        edge = jnp.dot(w_first, taps(xe), preferred_element_type=jnp.float32)
        for k in range(2):
            part = slice(k * cols, (k + 1) * cols)
            value = silu(main[:, part] + cond[...])
            side = silu(edge[:, part] + cond[...]) * side_ok
            if y + k == 0:
                value, side = value * up_ok.astype(jnp.float32), side * up_ok.astype(jnp.float32)
            if y + k == rows + 1:
                value, side = value * down_ok.astype(jnp.float32), side * down_ok.astype(jnp.float32)
            before = jnp.where(wide_lane == 0, side, pltpu.roll(value, 1, 1))
            after = jnp.where(wide_lane == cols - 1, side, pltpu.roll(value, cols - 1, 1))
            here = slice((y + k) * cols, (y + k + 1) * cols)
            hc[0:hidden, here] = before.astype(jnp.bfloat16)
            hc[hidden : 2 * hidden, here] = value.astype(jnp.bfloat16)
            hc[2 * hidden : 3 * hidden, here] = after.astype(jnp.bfloat16)

    def net_message(p):
        part = net.at[me, 2 * p : 2 * p + 2]
        return remote(part, part, NET + p, {"chan": other})

    def second_section(y):
        total = None
        for i in range(3):
            w = jnp.concatenate([w_mid[3 * i + j] for j in range(3)], axis=1)
            term = jnp.dot(
                w, hc[:, (y + i) * cols : (y + i + 2) * cols], preferred_element_type=jnp.float32
            )
            total = term if total is None else total + term
        wide = jnp.concatenate([bias_mid_col[...]] * 2, axis=1)
        middle = silu(total + wide).astype(jnp.bfloat16)
        out = jnp.dot(w_out, middle, preferred_element_type=jnp.float32)
        for k in range(2):
            net[me, y + k] = out[:, k * cols : (k + 1) * cols]

    each((LEFT, RIGHT), lambda d: message(BACK[d]).wait_recv())
    for r in range(HALO, rows + HALO):
        prepare(r)
    send_aux.wait_recv()
    w_out = jnp.concatenate([aux[0, 0:16], aux[1, 0:16]], axis=1).astype(jnp.bfloat16)
    bias_mid_col[...] = column(jnp.concatenate([aux[0, 16:17], aux[1, 16:17]], axis=1))
    own_weights.wait()
    send_weights.wait_recv()

    first_section(2)
    for y in range(2, rows - 2, 2):
        first_section(y + 2)
        second_section(y)
    for p in range(1, rows // 2 - 1):
        net_message(p).start()
    each((UP, DOWN, UL, UR, DL, DR), lambda d: message(BACK[d]).wait_recv())
    for r in [*range(HALO), *range(rows + HALO, ext)]:
        prepare(r)
    first_section(0)
    first_section(rows)
    second_section(0)
    second_section(rows - 2)
    for p in (0, rows // 2 - 1):
        net_message(p).start()

    def finish(s):
        now, later = levels(s)
        variance = now * now + sigma_data * sigma_data
        scale_now = jnp.sqrt(variance)
        keep = sigma_data * sigma_data / variance * scale_now
        gain = sigma_data * now / scale_now
        for c in range(channels):
            denoised_ref[s, c] = keep * latent_ref[s, c] + gain * net[s, :, c, :]

    finish(me)
    stores[3].start()
    for p in range(rows // 2):
        net_message(p).wait_recv()
    finish(other)
    stores[4].start()

    for d in range(8):
        @pl.when(exists(d))
        def _(d=d):
            message(d).wait_send()
    for d in (LEFT, RIGHT):
        @pl.when(exists(d))
        def _(d=d):
            coarse_message(d).wait_send()
    send_aux.wait_send()
    send_weights.wait_send()
    for p in range(rows // 2):
        net_message(p).wait_send()
    for store in stores:
        store.wait()


def on_device(
    latent, fresh_noise, step_index, coarse, weight_in, bias_in, weight_noise,
    weight_mid, bias_mid, weight_out,
):
    samples, channels, rows, cols = latent.shape
    coarse_rows, coarse_here = coarse.shape[1], coarse.shape[2]
    hidden = weight_in.shape[1]
    ext = rows + 2 * HALO
    stacked = -(-coarse_rows * GROUP // 128) * 128
    sizes = (lax.axis_size("row"), lax.axis_size("col"), cols // coarse_here)
    f32, bf16 = jnp.float32, jnp.bfloat16
    specs = [pl.BlockSpec(memory_space=pltpu.HBM)] * 10
    out_shapes = [latent.shape, latent.shape[1:], latent.shape, latent.shape]
    denoised, mean, noise, shrink = pl.pallas_call(
        functools.partial(kernel, sizes),
        out_shape=[jax.ShapeDtypeStruct(shape, f32) for shape in out_shapes],
        in_specs=specs,
        out_specs=[pl.BlockSpec(memory_space=pltpu.HBM)] * 4,
        scratch_shapes=[
            *[pltpu.VMEM(shape, f32) for shape in out_shapes],
            pltpu.SemaphoreType.DMA((5,)),
            pltpu.VMEM(latent.shape, f32),
            pltpu.VMEM(latent.shape, f32),
            pltpu.SMEM(step_index.shape, jnp.int32),
            pltpu.VMEM(coarse.shape, f32),
            pltpu.VMEM((9, weight_in.shape[2], hidden), bf16),
            pltpu.VMEM((1, hidden), f32),
            pltpu.VMEM((1, hidden), f32),
            pltpu.VMEM((1, hidden // 2), f32),
            pltpu.VMEM(weight_out.shape, bf16),
            pltpu.SemaphoreType.DMA((9,)),
            pltpu.VMEM((ext, GROUP, cols), f32),
            pltpu.VMEM((9, GROUP, cols), f32),
            pltpu.VMEM((coarse_here + 2 * EDGE, stacked), f32),
            pltpu.VMEM((stacked, 128), f32),
            pltpu.VMEM((2, 24, hidden // 2), f32),
            pltpu.VMEM((9, hidden, hidden), bf16),
            pltpu.VMEM((256, hidden), f32),
            pltpu.VMEM((BLOCK, ext * cols), bf16),
            pltpu.VMEM((BLOCK, ext * cols), bf16),
            pltpu.VMEM((3 * hidden, (rows + 2) * cols), bf16),
            pltpu.VMEM((samples, rows, 16, cols), f32),
            pltpu.VMEM((stacked, 6 * cols), f32),
            pltpu.VMEM((hidden, cols), f32),
            pltpu.VMEM((hidden, cols), f32),
            pltpu.SemaphoreType.DMA((12 + rows // 2,)),
            pltpu.SemaphoreType.DMA((12 + rows // 2,)),
            pltpu.SemaphoreType.DMA,
        ],
        compiler_params=pltpu.CompilerParams(
            collective_id=0, has_side_effects=True, vmem_limit_bytes=64 * 1024 * 1024
        ),
        name="denoise_step",
    )(
        latent, fresh_noise, step_index, coarse, jnp.transpose(weight_in, (0, 2, 1)), bias_in.reshape(1, hidden),
        weight_noise.reshape(1, hidden), weight_mid, bias_mid.reshape(1, hidden // 2), weight_out,
    )
    return mean[None] + denoised, denoised * shrink + noise


def solution(mesh):
    in_specs = (
        P("ens", None, "row", "col"),
        P("ens", None, "row", "col"),
        P("ens"),
        P("ens", None, "col"),
        P(),
        P(),
        P(),
        P(None, "chan", None),
        P("chan"),
        P(None, "chan"),
    )
    out_specs = (P("ens", None, "row", "col"), P("ens", None, "row", "col"))
    return jax.shard_map(
        on_device, mesh=mesh, in_specs=in_specs, out_specs=out_specs, check_vma=False
    )
```
